32 devices in a mesh: group: 4 (over y, core), space: 8 (over z, x).
Axes of the slice: x: 2, y: 2, z: 4, core: 2. Of those that a mesh axis runs over, the one named last changes fastest.
Arguments:
- initial_state: float32 [32, 3, 32, 1024], P(('group', 'space')), may hold values from -3 to 3
- phases: int32 [32, 32, 1024], P(('group', 'space')), may hold values from 0 to 2
- brick_coords: int32 [32, 3], P(('group', 'space')), may hold values from -1 to 7, as said below
- neighbours: int32 [32, 6], P(('group', 'space')), may hold values from -1 to 31, as said below
- source: float32 [32, 3, 32, 1024], P(('group', 'space'))
- coarse_inverse: float32 [4, 24, 24], P('group', 'space')
Outputs:
- final_state: float32 [32, 3, 32, 1024], P(('group', 'space'))
The draws below stay inside these ranges and needn't reach their ends.
Inputs may be any that keep to these rules, and one draw needn't show every extreme that they name: `brick_coords`: an occupied slot of device (g, s) holds the brick at x place bx, y = s, z = g; each x place occurs at most once on a device; an empty slot is -1 in all three; device (0, 0), every device with s = 7, and device (3, 6) have every slot occupied. Global slot = device index (group index * 8 + space index) + slot. The -x and +x neighbours lie on the same device, -y and +y on the device one step lower or higher along space, -z and +z one step lower or higher along group, always at the same x place; a face has a neighbour exactly where that brick is occupied; the relation is symmetric; empty slots have -1 everywhere.
All inputs are finite; a program needn't handle non-finite values.
Results may differ from the reference program's by a relative error of at most 0.0003.
Values sent between devices are 32-bit elements; how exact they have to be, the bound alone decides.
A program may use at most 64 MiB of HBM per device.

```python
import jax
import jax.numpy as jnp
from jax import lax

E = 32
BRICK_DEV = 1
NEWTON = 2
SMOOTH = 4
GROUPS = 4
COLUMNS = 8
GROUP_SLOTS = 8
SLOTS = 32


def brick_layout(key):
    first_key, second_key, third_key = jax.random.split(key, 3)
    shape = (GROUPS, COLUMNS, BRICK_DEV)
    share = jax.random.randint(first_key, (GROUPS, COLUMNS, 1), 40, 101)
    group_place = lax.broadcasted_iota(jnp.int32, (GROUPS, COLUMNS, 1), 0)
    column_place = lax.broadcasted_iota(jnp.int32, (GROUPS, COLUMNS, 1), 1)
    corner = (group_place + column_place == 0) | (column_place == COLUMNS - 1) | (column_place == COLUMNS - 2) & (group_place == GROUPS - 1)
    rolls = jax.random.randint(second_key, shape, 0, 100)
    filled = (rolls < share) | corner
    scores = jax.random.randint(third_key, shape, 0, 1 << 20) * BRICK_DEV + lax.broadcasted_iota(jnp.int32, shape, 2)
    order = jnp.argsort(scores, axis=2, stable=True).astype(jnp.int32)
    place = jnp.argsort(order, axis=2, stable=True).astype(jnp.int32)
    return (filled, order, place)


def shifted(values, axis, step, fill):
    size = values.shape[axis]
    padding = jnp.full_like(lax.slice_in_dim(values, 0, 1, axis=axis), fill)
    if step > 0:
        return jnp.concatenate([padding, lax.slice_in_dim(values, 0, size - 1, axis=axis)], axis)
    return jnp.concatenate([lax.slice_in_dim(values, 1, size, axis=axis), padding], axis)


def draw_brick_coords(key, part):
    filled, order, place = brick_layout(jax.random.fold_in(key, 11))
    taken = jnp.take_along_axis(filled, order, axis=2)
    shape = (GROUPS, COLUMNS, BRICK_DEV)
    column_index = lax.broadcasted_iota(jnp.int32, shape, 1)
    group_index = lax.broadcasted_iota(jnp.int32, shape, 0)
    placed = jnp.stack([order, column_index, group_index], -1)
    placed = jnp.where(taken[..., None], placed, -1)
    return placed.reshape(SLOTS, 3).astype(jnp.int32)


def draw_neighbours(key, part):
    filled, order, place = brick_layout(jax.random.fold_in(key, 11))
    taken = jnp.take_along_axis(filled, order, axis=2)
    device = lax.broadcasted_iota(jnp.int32, (GROUPS, COLUMNS, 1), 0) * COLUMNS + lax.broadcasted_iota(jnp.int32, (GROUPS, COLUMNS, 1), 1)
    result = []
    for axis, step, offset in ((2, 1, 0), (2, -1, 0), (1, 1, -1), (1, -1, 1), (0, 1, -COLUMNS), (0, -1, COLUMNS)):
        other_filled = jnp.take_along_axis(shifted(filled, axis, step, False), order, axis=2)
        other_slot = jnp.take_along_axis(shifted(place, axis, step, 0), order, axis=2)
        linked = (device + offset) * BRICK_DEV + other_slot
        result.append(jnp.where(taken & other_filled, linked, -1))
    return jnp.stack(result, -1).reshape(SLOTS, 6).astype(jnp.int32)


def draw_source(key, part):
    shape = (SLOTS, 3, E, E * E)
    first_key = jax.random.fold_in(jax.random.fold_in(key, 23), 0)
    position = lax.broadcasted_iota(jnp.float32, (SLOTS, 1, 1, 1), 0) / float(SLOTS - 1)
    scale = 0.3 * jnp.power(10.0, position)
    base = jax.random.normal(first_key, shape, jnp.float32)
    return (base * scale).astype(jnp.float32)


def draw_coarse_inverse(key, part):
    order_size = 3 * GROUP_SLOTS
    noise_key = jax.random.fold_in(key, 37)
    shape = (GROUPS, order_size, order_size)
    noise = jax.random.normal(noise_key, shape, jnp.float32)
    identity = (lax.broadcasted_iota(jnp.int32, shape, 1) == lax.broadcasted_iota(jnp.int32, shape, 2)).astype(jnp.float32)
    return ((identity + 0.5 * noise / jnp.sqrt(float(order_size))) / float(E * E)).astype(jnp.float32)


def place_ends(values, stream_key, smallest, largest):
    spot = [jax.random.randint(jax.random.fold_in(stream_key, axis), (), 0, length) for axis, length in enumerate(values.shape)]
    longest = values.shape.index(max(values.shape))
    beside = spot[:longest] + [(spot[longest] + 1) % values.shape[longest]] + spot[longest + 1:]
    return values.at[tuple(spot)].set(smallest).at[tuple(beside)].set(largest)


def block_scale(rng, dims, cuts, smallest, largest):
    def one(dim, shards_of):
        heights = jax.random.uniform(jax.random.fold_in(jax.random.fold_in(rng, 6), dim), (shards_of,), jnp.float32, smallest / len(cuts), largest / len(cuts))
        return jnp.repeat(jnp.exp(heights), dims[dim] // shards_of).reshape((-1,) + (1,) * (len(dims) - dim - 1))

    factor_of = one(*cuts[0])
    for cut in cuts[1:]:
        factor_of = factor_of * one(*cut)
    return factor_of


def scatter_about(stream_key, dims, deviation, most, cuts=(), held_as=jnp.bfloat16):
    values = deviation * jax.random.normal(stream_key, dims, jnp.float32)
    if cuts:
        values = values * block_scale(stream_key, dims, cuts, -0.22, 0.18)
    return jnp.clip(values, -most, most).astype(held_as)


def setup_inputs(seed: int = 0) -> dict:
    key_of = jax.random.split(jax.random.key(seed), 7)
    initial_state = scatter_about(key_of[0], (SLOTS, 3, E, E * E), 0.5, 3.0, ((0, 32),), jnp.float32)
    phases = place_ends(jax.random.randint(key_of[1], (SLOTS, E, E * E), 0, 3), jax.random.fold_in(key_of[1], 1), 0, 2).astype(jnp.int32)
    brick_coords = draw_brick_coords(jax.random.fold_in(key_of[6], 71), 0)
    neighbours = draw_neighbours(jax.random.fold_in(key_of[6], 71), 0)
    source = draw_source(jax.random.fold_in(key_of[6], 71), 0)
    coarse_inverse = draw_coarse_inverse(jax.random.fold_in(key_of[6], 71), 0)
    return dict(initial_state=initial_state, phases=phases, brick_coords=brick_coords, neighbours=neighbours, source=source, coarse_inverse=coarse_inverse)


SHIFT_TERM = 0.5
BETA_SLOPE = 0.5
ALPHA_SHARE = 0.5
LITHIUM_RATE = 0.5
OMEGA_DAMP = 0.8
CONDUCT_TABLE = ((1.0, 0.2, 0.2), (1.0, 0.1, 0.1), (0.05, 0.5, 1.5))
RATE_TABLE = (0.0, 0.3, 0.02)

def coefficients(phases):
    conductance = jnp.zeros((phases.shape[0], 3) + phases.shape[1:], jnp.float32)
    rates = jnp.zeros((phases.shape[0], 1) + phases.shape[1:], jnp.float32)
    for label in range(3):
        landed = (phases == label).astype(jnp.float32)[:, None]
        column = jnp.array([CONDUCT_TABLE[0][label], CONDUCT_TABLE[1][label], CONDUCT_TABLE[2][label]], jnp.float32)
        conductance = conductance + landed * column[None, :, None, None]
        rates = rates + landed * RATE_TABLE[label]
    return (conductance, rates)

def face_planes(field):
    slots_here, fields, edge_cells, lanes = field.shape
    cube = field.reshape(slots_here, fields, edge_cells, edge_cells, edge_cells)
    return (field[:, :, 0, :], field[:, :, -1, :], field[..., :edge_cells].reshape(slots_here, fields, lanes), field[..., lanes - edge_cells:].reshape(slots_here, fields, lanes), cube[..., 0].reshape(slots_here, fields, lanes), cube[..., -1].reshape(slots_here, fields, lanes))

def neighbour_sum(field, ghosts):
    lower_x, upper_x, lower_y, upper_y, lower_z, upper_z = ghosts
    slots_here, fields, edge_cells, lanes = field.shape
    along_x = jnp.concatenate([field[:, :, 1:], upper_x[:, :, None]], 2) + jnp.concatenate([lower_x[:, :, None], field[:, :, :-1]], 2)
    along_y = jnp.concatenate([field[..., edge_cells:], upper_y.reshape(slots_here, fields, edge_cells, edge_cells)], 3)
    along_y = along_y + jnp.concatenate([lower_y.reshape(slots_here, fields, edge_cells, edge_cells), field[..., :lanes - edge_cells]], 3)
    depth = lax.broadcasted_iota(jnp.int32, (1, 1, 1, lanes), 3) % edge_cells

    def spread(plane):
        return jnp.broadcast_to(plane.reshape(slots_here, fields, edge_cells, edge_cells, 1), (slots_here, fields, edge_cells, edge_cells, edge_cells)).reshape(slots_here, fields, edge_cells, lanes)
    forward = jnp.where(depth == edge_cells - 1, spread(upper_z), jnp.concatenate([field[..., 1:], field[..., :1]], 3))
    backward = jnp.where(depth == 0, spread(lower_z), jnp.concatenate([field[..., -1:], field[..., :-1]], 3))
    return along_x + along_y + forward + backward

def place_ghosts(sources, neighbours, walls):
    result = []
    for direction in range(6):
        linked = neighbours[:, direction]
        usable = linked >= 0
        target = jnp.where(usable, linked, 0) % sources[direction].shape[0]
        picked = jnp.take(sources[direction], target, axis=0)
        result.append(jnp.where(usable[:, None, None], picked, walls[:, :, None]))
    return tuple(result)

def local_terms(state, around, conductance, rates, source, mask):
    lithium = state[:, 0:1]
    electrolyte = state[:, 1:2]
    solid_phase = state[:, 2:3]
    overpotential = solid_phase - electrolyte - BETA_SLOPE * lithium
    forward_rate = jnp.exp(ALPHA_SHARE * overpotential)
    backward_rate = jnp.exp(-ALPHA_SHARE * overpotential)
    current = rates * (forward_rate - backward_rate)
    slope_term = rates * ALPHA_SHARE * (forward_rate + backward_rate)
    reaction = jnp.concatenate([-LITHIUM_RATE * current, -current, current], 1)
    misfit = (SHIFT_TERM * state + conductance * (6.0 * state - around) + reaction - source) * mask
    return (misfit, slope_term)

def linear_image(update, around, conductance, slope_term, mask):
    coupled = slope_term * (update[:, 2:3] - update[:, 1:2] - BETA_SLOPE * update[:, 0:1])
    reaction = jnp.concatenate([-LITHIUM_RATE * coupled, -coupled, coupled], 1)
    return (SHIFT_TERM * update + conductance * (6.0 * update - around) + reaction) * mask

def diagonal_of(conductance, slope_term):
    reaction = jnp.concatenate([LITHIUM_RATE * BETA_SLOPE * slope_term, slope_term, slope_term], 1)
    return SHIFT_TERM + 6.0 * conductance + reaction

def gather_around(field, neighbours, walls):
    faces = face_planes(field)
    sources = (faces[1], faces[0], faces[3], faces[2], faces[5], faces[4])
    return neighbour_sum(field, place_ghosts(sources, neighbours, walls))

def reference(initial_state, phases, brick_coords, neighbours, source, coarse_inverse):
    mask = (brick_coords[:, 0] >= 0).astype(jnp.float32)[:, None, None, None]
    conductance, rates = coefficients(phases)
    placed = brick_coords.astype(jnp.float32)
    wall_phi = placed[:, 0] / BRICK_DEV + placed[:, 1] / COLUMNS + placed[:, 2] / GROUPS - 1.0
    blank = jnp.zeros_like(wall_phi)
    walls = jnp.stack([blank, blank, wall_phi], 1)
    zero_walls = jnp.zeros_like(walls)
    state = initial_state * mask
    total_cells = 3.0 * SLOTS * E * E * E
    for sweep_index in range(NEWTON):
        misfit, slope_term = local_terms(state, gather_around(state, neighbours, walls), conductance, rates, source, mask)
        squares = jnp.sum(misfit * misfit)
        diagonal = diagonal_of(conductance, slope_term)

        def apply_jacobian(update):
            return linear_image(update, gather_around(update, neighbours, zero_walls), conductance, slope_term, mask)
        update = OMEGA_DAMP * -misfit / diagonal
        for pass_index in range(SMOOTH - 1):
            update = update + OMEGA_DAMP * (-misfit - apply_jacobian(update)) / diagonal
        leftover = -misfit - apply_jacobian(update)
        coarse_residual = lax.optimization_barrier(jnp.sum(leftover, axis=(2, 3))).reshape(GROUPS, 3 * GROUP_SLOTS)
        correction = jnp.einsum('gij,gj->gi', coarse_inverse, coarse_residual, precision=lax.Precision.HIGHEST)
        update = update + correction.reshape(SLOTS, 3)[:, :, None, None] * mask
        damping = 1.0 / (1.0 + jnp.sqrt(squares / total_cells + 1e-06))
        state = state + damping * update
    return state
```

```python
import functools

import jax
import jax.numpy as jnp
from jax import lax
from jax.experimental import pallas as pl
from jax.experimental.pallas import tpu as pltpu
from jax.sharding import PartitionSpec as P

NEWTON = 2
SMOOTH = 4
ROUNDS = SMOOTH + 1
E = 32
TILES = 8
PAD = 8
OMEGA = 0.8
MESH = pl.DeviceIdType.MESH
F32 = jnp.float32


def roll(x, shift):
    shift = shift % 128
    return x if shift == 0 else pltpu.roll(x, shift, 1)


def place(f, t):
    return (0, 16 * f + 2 * t) if f < 2 else (1, 2 * t)


def kernel(
    n, m,
    coords, links, inverse, state_in, phase_in, source_in, out,
    state, upd, base, gain, mix, diag, source, phase,
    send, recv, squares_a, squares_b, coarse, weights,
    face_send, face_recv, a_send, a_recv, b_send, b_recv, c_send, c_recv,
):
    me_s = lax.axis_index("space")
    me_g = lax.axis_index("group")
    lane = lax.broadcasted_iota(jnp.int32, (E, 128), 1)
    block = lane // 32
    depth = lane % 32
    first = depth == 0
    last = depth == 31
    edge = first | last
    even = lane % 2 == 0

    targets = (("space", me_s, 1, n), ("space", me_s, -1, n), ("group", me_g, 1, m), ("group", me_g, -1, m))

    def has(axis, me, step, size):
        return me + step < size if step > 0 else me + step >= 0

    barrier = pltpu.get_barrier_semaphore()
    for axis, me, size in (("space", me_s, n), ("group", me_g, m)):
        for d in range(1, size):
            pl.semaphore_signal(barrier, inc=1, device_id={axis: lax.rem(me + d, size)}, device_id_type=MESH)

    def face_copy(r, d):
        axis, me, step, size = targets[d]
        return pltpu.make_async_remote_copy(
            src_ref=send.at[r, d], dst_ref=recv.at[r, d],
            send_sem=face_send.at[r, d], recv_sem=face_recv.at[r, d],
            device_id={axis: jnp.clip(me + step, 0, size - 1)}, device_id_type=MESH)

    def source_of(d):
        axis, me, step, size = targets[d]
        return has(axis, me, -step, size)

    def start_faces(r):
        for d in range(4):
            @pl.when(has(*targets[d]))
            def _():
                face_copy(r, d).start()

    def wait_faces(r):
        for d in range(4):
            @pl.when(source_of(d))
            def _():
                face_copy(r, d).wait_recv()

    def gather_copy(buf, ss, rs, k, d, axis, me, size):
        return pltpu.make_async_remote_copy(
            src_ref=buf.at[k, 0], dst_ref=buf.at[k, d],
            send_sem=ss.at[k, d], recv_sem=rs.at[k, d],
            device_id={axis: lax.rem(me + d, size)}, device_id_type=MESH)

    over_a = (squares_a, a_send, a_recv)
    over_b = (squares_b, b_send, b_recv)
    over_c = (coarse, c_send, c_recv)

    def gather_start(bufs, k, axis, me, size):
        for d in range(1, size):
            gather_copy(*bufs, k, d, axis, me, size).start()

    def gather_wait(bufs, k, axis, me, size):
        for d in range(1, size):
            gather_copy(*bufs, k, d, axis, me, size).wait_recv()


    def swap4(a):
        low = block < 2
        t0 = jnp.where(low, a[0], roll(a[2], 64))
        t2 = jnp.where(low, roll(a[0], 64), a[2])
        t1 = jnp.where(low, a[1], roll(a[3], 64))
        t3 = jnp.where(low, roll(a[1], 64), a[3])
        ev = block % 2 == 0
        return (jnp.where(ev, t0, roll(t1, 32)), jnp.where(ev, roll(t0, 96), t1),
                jnp.where(ev, t2, roll(t3, 32)), jnp.where(ev, roll(t2, 96), t3))

    def spread_in(load):
        tiles = [None] * 8
        for h in range(2):
            got = swap4([load(2 * k + h) for k in range(4)])
            for r in range(4):
                tiles[4 * h + r] = got[r]
        return tiles

    occupied = coords[0, 0] >= 0
    mask = jnp.where(occupied, 1.0, 0.0).astype(F32)
    wall = coords[0, 0].astype(F32) + coords[0, 1].astype(F32) / n + coords[0, 2].astype(F32) / m - 1.0
    linked = [links[0, 2 + d] >= 0 for d in range(4)]

    zero_rows = jnp.zeros((PAD, 128), F32)
    for f in range(3):
        for t in range(TILES):
            edge_rows = zero_rows if f < 2 else zero_rows + wall
            state[f, t, 0:PAD] = edge_rows
            state[f, t, PAD + E:] = edge_rows
            for b in range(2):
                upd[b, f, t, 0:PAD] = zero_rows
                upd[b, f, t, PAD + E:] = zero_rows
    for f in range(3):
        tiles = spread_in(lambda t: state_in[f, :, t * 128:(t + 1) * 128])
        for t in range(TILES):
            state[f, t, PAD:PAD + E] = tiles[t] * mask

    def pack_z(planes, f, t, c):
        q, j = place(f, t)
        part = roll(jnp.where(edge, c, 0.0), j)
        planes[q] = part if planes[q] is None else planes[q] + part

    def post_faces(r, planes, ends):
        q0, q1 = planes
        send[r, 3] = jnp.where(even, q0, roll(q1, 1))
        send[r, 2] = jnp.where(even, roll(q1, -1), q0)
        up = jnp.where(block == 0, roll(ends[0][1], -96), jnp.where(block == 1, roll(ends[1][1], -64), roll(ends[2][1], -32)))
        down = jnp.where(block == 0, ends[0][0], jnp.where(block == 1, roll(ends[1][0], 32), roll(ends[2][0], 64)))
        send[r, 0] = up
        send[r, 1] = down
        start_faces(r)

    def ghosts_of(r, walls):
        wait_faces(r)
        got = [recv[r, d] for d in range(4)]
        y_low, y_high, z_low, z_high = got
        if walls:
            plain = [jnp.where(linked[d], got[d], 0.0) for d in range(4)]
            solid = [jnp.where(linked[d], got[d], wall) for d in range(4)]
        else:
            plain = solid = got
        c0 = jnp.where(even, plain[3], roll(plain[2], 66))
        c1 = jnp.where(even, roll(solid[3], -1), roll(solid[2], 67))
        lows = [roll((plain if f < 2 else solid)[0], -32 * f) for f in range(3)]
        highs = [roll((plain if f < 2 else solid)[1], 96 - 32 * f) for f in range(3)]
        return (c0, c1), lows, highs

    def around(ref, f, t, ghosts):
        planes, lows, highs = ghosts
        c = ref[f, t, PAD:PAD + E]
        total = ref[f, t, PAD - 1:PAD - 1 + E] + ref[f, t, PAD + 1:PAD + 1 + E]
        if t > 0:
            total = total + ref[f, t - 1, PAD:PAD + E]
        else:
            total = total + jnp.where(block == 0, lows[f], roll(ref[f, TILES - 1, PAD:PAD + E], 32))
        if t < TILES - 1:
            total = total + ref[f, t + 1, PAD:PAD + E]
        else:
            total = total + jnp.where(block == 3, highs[f], roll(ref[f, 0, PAD:PAD + E], -32))
        q, j = place(f, t)
        ghost = roll(planes[q], 31 - j)
        total = total + jnp.where(last, ghost, roll(c, -1)) + jnp.where(first, ghost, roll(c, 1))
        return c, total

    def post_state(r):
        planes, ends = [None, None], []
        for f in range(3):
            tiles = [state[f, t, PAD:PAD + E] for t in range(TILES)]
            for t in range(TILES):
                pack_z(planes, f, t, tiles[t])
            ends.append((tiles[0], tiles[TILES - 1]))
        post_faces(r, planes, ends)

    pl.semaphore_wait(barrier, n + m - 2)
    post_state(0)

    rows8 = lax.broadcasted_iota(jnp.int32, (8, 128), 0)
    blank = jnp.zeros((E, 128), F32)
    for d in range(4):
        @pl.when(jnp.logical_not(source_of(d)))
        def _():
            for r in range(NEWTON * ROUNDS):
                recv[r, d] = blank
    for f in range(3):
        tiles = spread_in(lambda t: source_in[f, :, t * 128:(t + 1) * 128])
        for t in range(TILES):
            source[f, t] = tiles[t]
    tiles = spread_in(lambda t: phase_in[:, t * 128:(t + 1) * 128])
    for t in range(TILES):
        phase[t] = tiles[t]
    for d in range(n):
        owner = lax.rem(me_s - d + n, n)
        for i in range(3):
            v = [inverse[0, i, 3 * owner + f] for f in range(3)]
            weights[i, d] = jnp.where(rows8 == 0, v[0], jnp.where(rows8 == 1, v[1], jnp.where(rows8 == 2, v[2], 0.0)))

    def fold(x):
        return x[0:8] + x[8:16] + x[16:24] + x[24:32]

    def sweep(k, carry):
        r0 = k * ROUNDS
        ghosts = ghosts_of(r0, True)
        planes, ends = [None, None], [[None, None] for _ in range(3)]
        square = jnp.zeros((E, 128), F32)
        for t in range(TILES):
            label = phase[t]
            pore = label == 0
            active = label == 1
            conduct = (jnp.where(pore, 1.0, 0.2), jnp.where(pore, 1.0, 0.1),
                       jnp.where(pore, 0.05, jnp.where(active, 0.5, 1.5)))
            rates = jnp.where(pore, 0.0, jnp.where(active, 0.3, 0.02))
            pairs = [around(state, f, t, ghosts) for f in range(3)]
            c, e, s = (p[0] for p in pairs)
            eta = s - e - 0.5 * c
            forward = jnp.exp(0.5 * eta)
            backward = jnp.exp(-0.5 * eta)
            current = rates * (forward - backward)
            slope = 0.5 * rates * (forward + backward)
            react = (-0.5 * current, -current, current)
            for f in range(3):
                v, total = pairs[f]
                misfit = mask * (0.5 * v + conduct[f] * (6.0 * v - total) + react[f] - source[f, t])
                square = square + misfit * misfit
                dg = 0.5 + 6.0 * conduct[f] + (0.25 * slope if f == 0 else slope)
                w = (OMEGA * mask) / dg
                b = -w * misfit
                base[f, t] = b
                upd[0, f, t, PAD:PAD + E] = b
                gain[f, t] = w * conduct[f]
                mix[f, t] = w * slope * (0.5 if f == 0 else 1.0)
                diag[f, t] = dg * (1.0 / OMEGA)
                pack_z(planes, f, t, b)
                if t == 0:
                    ends[f][0] = b
                if t == TILES - 1:
                    ends[f][1] = b
        post_faces(r0 + 1, planes, ends)
        squares_a[k, 0] = fold(square)
        gather_start(over_a, k, "space", me_s, n)

        def terms(u, t, ghosts):
            pairs = [around(u, f, t, ghosts) for f in range(3)]
            c, e, s = (p[0] for p in pairs)
            half = 0.5 * c
            cross = (s - e, s - half, e + half)
            return [(pairs[f][0], base[f, t] + gain[f, t] * pairs[f][1] + mix[f, t] * cross[f]) for f in range(3)]

        def smooth(p, carry):
            now = lax.rem(p, 2)
            u, later = upd.at[now], upd.at[1 - now]
            ghosts = ghosts_of(r0 + 1 + p, False)
            planes, ends = [None, None], [[None, None] for _ in range(3)]
            for t in range(TILES):
                for f, (v, term) in enumerate(terms(u, t, ghosts)):
                    value = (1.0 - OMEGA) * v + term
                    later[f, t, PAD:PAD + E] = value
                    pack_z(planes, f, t, value)
                    if t == 0:
                        ends[f][0] = value
                    if t == TILES - 1:
                        ends[f][1] = value
            post_faces(r0 + 2 + p, planes, ends)
            return carry

        lax.fori_loop(0, 1, smooth, 0)
        gather_wait(over_a, k, "space", me_s, n)
        part = squares_a[k, 0]
        for d in range(1, n):
            part = part + squares_a[k, d]
        squares_b[k, 0] = part
        gather_start(over_b, k, "group", me_g, m)
        lax.fori_loop(1, SMOOTH - 1, smooth, 0)

        u = upd.at[(SMOOTH - 1) % 2]
        ghosts = ghosts_of(r0 + SMOOTH, False)
        sums = [jnp.zeros((E, 128), F32) for _ in range(3)]
        for t in range(TILES):
            for f, (v, term) in enumerate(terms(u, t, ghosts)):
                sums[f] = sums[f] + diag[f, t] * (term - OMEGA * v)
        rows = [jnp.sum(x, axis=0, keepdims=True) for x in sums]
        coarse[k, 0] = jnp.where(rows8 == 0, rows[0], jnp.where(rows8 == 1, rows[1], jnp.where(rows8 == 2, rows[2], 0.0)))
        gather_start(over_c, k, "space", me_s, n)

        gather_wait(over_b, k, "group", me_g, m)
        part = squares_b[k, 0]
        for d in range(1, m):
            part = part + squares_b[k, d]
        whole = jnp.sum(jnp.sum(part, axis=0, keepdims=True), axis=1, keepdims=True)
        cells = 3.0 * n * m * E * E * E
        damping = 1.0 / (1.0 + jnp.sqrt(whole / cells + 1e-6))

        gather_wait(over_c, k, "space", me_s, n)
        got = [coarse[k, d] for d in range(n)]
        planes, ends = [None, None], [[None, None] for _ in range(3)]
        for f in range(3):
            acc = got[0] * weights[f, 0]
            for d in range(1, n):
                acc = acc + got[d] * weights[f, d]
            lift = mask * jnp.sum(jnp.sum(acc, axis=0, keepdims=True), axis=1, keepdims=True)
            for t in range(TILES):
                value = state[f, t, PAD:PAD + E] + damping * (u[f, t, PAD:PAD + E] + lift)
                state[f, t, PAD:PAD + E] = value
                pack_z(planes, f, t, value)
                if t == 0:
                    ends[f][0] = value
                if t == TILES - 1:
                    ends[f][1] = value

        @pl.when(k < NEWTON - 1)
        def _():
            post_faces(r0 + ROUNDS, planes, ends)

        return carry

    lax.fori_loop(0, NEWTON, sweep, 0)

    for f in range(3):
        for h in range(2):
            got = swap4([state[f, 4 * h + r, PAD:PAD + E] for r in range(4)])
            for k in range(4):
                t = 2 * k + h
                out[f, :, t * 128:(t + 1) * 128] = got[k]

    for r in range(NEWTON * ROUNDS):
        for d in range(4):
            @pl.when(has(*targets[d]))
            def _():
                face_copy(r, d).wait_send()
    for k in range(NEWTON):
        for bufs, axis, me, size in ((over_a, "space", me_s, n), (over_b, "group", me_g, m), (over_c, "space", me_s, n)):
            for d in range(1, size):
                gather_copy(*bufs, k, d, axis, me, size).wait_send()


def shards(n, m, initial_state, phases, brick_coords, neighbours, source, coarse_inverse):
    rounds = NEWTON * ROUNDS
    smem = pl.BlockSpec(memory_space=pltpu.SMEM)
    vmem = pl.BlockSpec(memory_space=pltpu.VMEM)
    padded = (3, TILES, E + 2 * PAD, 128)
    inner = (3, TILES, E, 128)
    dma = pltpu.SemaphoreType.DMA
    result = pl.pallas_call(
        functools.partial(kernel, n, m),
        out_shape=jax.ShapeDtypeStruct((3, E, E * E), F32),
        in_specs=[smem, smem, smem, vmem, vmem, vmem],
        out_specs=vmem,
        scratch_shapes=[
            pltpu.VMEM(padded, F32),
            pltpu.VMEM((2,) + padded, F32),
            pltpu.VMEM(inner, F32),
            pltpu.VMEM(inner, F32),
            pltpu.VMEM(inner, F32),
            pltpu.VMEM(inner, F32),
            pltpu.VMEM(inner, F32),
            pltpu.VMEM(inner[1:], jnp.int32),
            pltpu.VMEM((rounds, 4, E, 128), F32),
            pltpu.VMEM((rounds, 4, E, 128), F32),
            pltpu.VMEM((NEWTON, n, 8, 128), F32),
            pltpu.VMEM((NEWTON, m, 8, 128), F32),
            pltpu.VMEM((NEWTON, n, 8, 128), F32),
            pltpu.VMEM((3, n, 8, 128), F32),
            dma((rounds, 4)), dma((rounds, 4)),
            dma((NEWTON, n)), dma((NEWTON, n)),
            dma((NEWTON, m)), dma((NEWTON, m)),
            dma((NEWTON, n)), dma((NEWTON, n)),
        ],
        compiler_params=pltpu.CompilerParams(
            collective_id=0, has_side_effects=True, vmem_limit_bytes=40 * 1024 * 1024
        ),
    )(brick_coords, neighbours, coarse_inverse, initial_state[0], phases[0], source[0])
    return result[None]


def solution(mesh):
    both = ("group", "space")
    return jax.shard_map(
        functools.partial(shards, mesh.shape["space"], mesh.shape["group"]),
        mesh=mesh,
        in_specs=(
            P(both, None, None, None),
            P(both, None, None),
            P(both, None),
            P(both, None),
            P(both, None, None, None),
            P("group", "space", None),
        ),
        out_specs=P(both, None, None, None),
        check_vma=False,
    )
```

```python
import functools

import jax
import jax.numpy as jnp
from jax import lax
from jax.experimental import pallas as pl
from jax.experimental.pallas import tpu as pltpu
from jax.sharding import PartitionSpec as P

NEWTON = 2
SMOOTH = 4
ROUNDS = SMOOTH + 1
E = 32
TILES = 8
PAD = 8
OMEGA = 0.8
MESH = pl.DeviceIdType.MESH
F32 = jnp.float32


def roll(x, shift):
    shift = shift % 128
    return x if shift == 0 else pltpu.roll(x, shift, 1)


def place(f, t):
    return (0, 16 * f + 2 * t) if f < 2 else (1, 2 * t)


def kernel(
    n, m,
    coords_in, links_in, inverse_in, state_hbm, phase_hbm, source_hbm, out,
    coords, links, inverse, state_in, phase_in, source_in, fetch,
    state, upd, base, gain, mix, diag, source, phase,
    send, recv, squares_a, squares_b, coarse, weights,
    face_send, face_recv, a_send, a_recv, b_send, b_recv, c_send, c_recv,
):
    me_s = lax.axis_index("space")
    me_g = lax.axis_index("group")
    lane = lax.broadcasted_iota(jnp.int32, (E, 128), 1)
    block = lane // 32
    depth = lane % 32
    first = depth == 0
    last = depth == 31
    edge = first | last
    even = lane % 2 == 0

    fetches = [
        pltpu.make_async_copy(a, b, fetch.at[i])
        for i, (a, b) in enumerate((
            (state_hbm, state_in), (coords_in, coords), (links_in, links),
            (phase_hbm, phase_in), (source_hbm, source_in), (inverse_in, inverse),
        ))
    ]
    for copy in fetches:
        copy.start()

    targets = (("space", me_s, 1, n), ("space", me_s, -1, n), ("group", me_g, 1, m), ("group", me_g, -1, m))

    def has(axis, me, step, size):
        return me + step < size if step > 0 else me + step >= 0

    barrier = pltpu.get_barrier_semaphore()
    for axis, me, size in (("space", me_s, n), ("group", me_g, m)):
        for d in range(1, size):
            pl.semaphore_signal(barrier, inc=1, device_id={axis: lax.rem(me + d, size)}, device_id_type=MESH)

    def face_copy(r, d):
        axis, me, step, size = targets[d]
        return pltpu.make_async_remote_copy(
            src_ref=send.at[r, d], dst_ref=recv.at[r, d],
            send_sem=face_send.at[r, d], recv_sem=face_recv.at[r, d],
            device_id={axis: jnp.clip(me + step, 0, size - 1)}, device_id_type=MESH)

    def source_of(d):
        axis, me, step, size = targets[d]
        return has(axis, me, -step, size)

    def start_faces(r, which):
        for d in which:
            @pl.when(has(*targets[d]))
            def _():
                face_copy(r, d).start()

    def wait_faces(r, which):
        for d in which:
            @pl.when(source_of(d))
            def _():
                face_copy(r, d).wait_recv()

    def gather_copy(buf, ss, rs, k, d, axis, me, size):
        return pltpu.make_async_remote_copy(
            src_ref=buf.at[k, 0], dst_ref=buf.at[k, d],
            send_sem=ss.at[k, d], recv_sem=rs.at[k, d],
            device_id={axis: lax.rem(me + d, size)}, device_id_type=MESH)

    over_a = (squares_a, a_send, a_recv)
    over_b = (squares_b, b_send, b_recv)
    over_c = (coarse, c_send, c_recv)

    def gather_start(bufs, k, axis, me, size):
        for d in range(1, size):
            gather_copy(*bufs, k, d, axis, me, size).start()

    def gather_wait(bufs, k, axis, me, size):
        for d in range(1, size):
            gather_copy(*bufs, k, d, axis, me, size).wait_recv()


    def swap4(a):
        low = block < 2
        t0 = jnp.where(low, a[0], roll(a[2], 64))
        t2 = jnp.where(low, roll(a[0], 64), a[2])
        t1 = jnp.where(low, a[1], roll(a[3], 64))
        t3 = jnp.where(low, roll(a[1], 64), a[3])
        ev = block % 2 == 0
        return (jnp.where(ev, t0, roll(t1, 32)), jnp.where(ev, roll(t0, 96), t1),
                jnp.where(ev, t2, roll(t3, 32)), jnp.where(ev, roll(t2, 96), t3))

    def spread_in(load):
        tiles = [None] * 8
        for h in range(2):
            got = swap4([load(2 * k + h) for k in range(4)])
            for r in range(4):
                tiles[4 * h + r] = got[r]
        return tiles

    fetches[1].wait()
    fetches[2].wait()
    occupied = coords[0, 0] >= 0
    mask = jnp.where(occupied, 1.0, 0.0).astype(F32)
    wall = coords[0, 0].astype(F32) + coords[0, 1].astype(F32) / n + coords[0, 2].astype(F32) / m - 1.0
    linked = [links[0, 2 + d] >= 0 for d in range(4)]

    zero_rows = jnp.zeros((PAD, 128), F32)
    for f in range(3):
        for t in range(TILES):
            edge_rows = zero_rows if f < 2 else zero_rows + wall
            state[f, t, 0:PAD] = edge_rows
            state[f, t, PAD + E:] = edge_rows
            for b in range(2):
                upd[b, f, t, 0:PAD] = zero_rows
                upd[b, f, t, PAD + E:] = zero_rows
    fetches[0].wait()
    for f in range(3):
        tiles = spread_in(lambda t: state_in[f, :, t * 128:(t + 1) * 128])
        for t in range(TILES):
            state[f, t, PAD:PAD + E] = tiles[t] * mask

    def pack_z(planes, f, t, c):
        q, j = place(f, t)
        part = roll(jnp.where(edge, c, 0.0), j)
        planes[q] = part if planes[q] is None else planes[q] + part

    def post_y(r, ends):
        up = jnp.where(block == 0, roll(ends[0][1], -96), jnp.where(block == 1, roll(ends[1][1], -64), roll(ends[2][1], -32)))
        down = jnp.where(block == 0, ends[0][0], jnp.where(block == 1, roll(ends[1][0], 32), roll(ends[2][0], 64)))
        send[r, 0] = up
        send[r, 1] = down
        start_faces(r, (0, 1))

    def post_z(r, planes):
        q0, q1 = planes
        send[r, 3] = jnp.where(even, q0, roll(q1, 1))
        send[r, 2] = jnp.where(even, roll(q1, -1), q0)
        start_faces(r, (2, 3))

    def walled(r, d, walls):
        got = recv[r, d]
        if not walls:
            return got, got
        return jnp.where(linked[d], got, 0.0), jnp.where(linked[d], got, wall)

    def ghosts_z(r, walls):
        wait_faces(r, (2, 3))
        low, solid_low = walled(r, 2, walls)
        high, solid_high = walled(r, 3, walls)
        c0 = jnp.where(even, high, roll(low, 66))
        c1 = jnp.where(even, roll(solid_high, -1), roll(solid_low, 67))
        return c0, c1

    def ghosts_y(r, walls):
        wait_faces(r, (0, 1))
        low = walled(r, 0, walls)
        high = walled(r, 1, walls)
        lows = [roll(low[f // 2], -32 * f) for f in range(3)]
        highs = [roll(high[f // 2], 96 - 32 * f) for f in range(3)]
        return lows, highs

    inside = tuple(range(1, TILES - 1))
    outside = (0, TILES - 1)

    def around(ref, f, t, ghosts):
        planes, (lows, highs) = ghosts
        c = ref[f, t, PAD:PAD + E]
        total = ref[f, t, PAD - 1:PAD - 1 + E] + ref[f, t, PAD + 1:PAD + 1 + E]
        if t > 0:
            total = total + ref[f, t - 1, PAD:PAD + E]
        else:
            total = total + jnp.where(block == 0, lows[f], roll(ref[f, TILES - 1, PAD:PAD + E], 32))
        if t < TILES - 1:
            total = total + ref[f, t + 1, PAD:PAD + E]
        else:
            total = total + jnp.where(block == 3, highs[f], roll(ref[f, 0, PAD:PAD + E], -32))
        q, j = place(f, t)
        ghost = roll(planes[q], 31 - j)
        total = total + jnp.where(last, ghost, roll(c, -1)) + jnp.where(first, ghost, roll(c, 1))
        return c, total

    def pack_state():
        planes, ends = [None, None], []
        for f in range(3):
            tiles = [state[f, t, PAD:PAD + E] for t in range(TILES)]
            for t in range(TILES):
                pack_z(planes, f, t, tiles[t])
            ends.append((tiles[0], tiles[TILES - 1]))
        return planes, ends

    planes, ends = pack_state()
    pl.semaphore_wait(barrier, n + m - 2)
    post_y(0, ends)
    post_z(0, planes)

    rows8 = lax.broadcasted_iota(jnp.int32, (8, 128), 0)
    blank = jnp.zeros((E, 128), F32)
    for d in range(4):
        @pl.when(jnp.logical_not(source_of(d)))
        def _():
            for r in range(NEWTON * ROUNDS):
                recv[r, d] = blank
    for copy in fetches[3:]:
        copy.wait()
    for f in range(3):
        tiles = spread_in(lambda t: source_in[f, :, t * 128:(t + 1) * 128])
        for t in range(TILES):
            source[f, t] = tiles[t]
    tiles = spread_in(lambda t: phase_in[:, t * 128:(t + 1) * 128])
    for t in range(TILES):
        phase[t] = tiles[t]
    for d in range(n):
        owner = lax.rem(me_s - d + n, n)
        for i in range(3):
            v = [inverse[i, 0, 3 * owner + f] for f in range(3)]
            weights[i, d] = jnp.where(rows8 == 0, v[0], jnp.where(rows8 == 1, v[1], jnp.where(rows8 == 2, v[2], 0.0)))

    def fold(x):
        return x[0:8] + x[8:16] + x[16:24] + x[24:32]

    def sweep(k, carry):
        r0 = k * ROUNDS
        planes_in = ghosts_z(r0, True)
        ghosts = (planes_in, (None, None))
        planes, ends = [None, None], [[None, None] for _ in range(3)]
        square = jnp.zeros((E, 128), F32)
        for t in inside + outside:
            if t == 0:
                ghosts = (planes_in, ghosts_y(r0, True))
            label = phase[t]
            pore = label == 0
            active = label == 1
            conduct = (jnp.where(pore, 1.0, 0.2), jnp.where(pore, 1.0, 0.1),
                       jnp.where(pore, 0.05, jnp.where(active, 0.5, 1.5)))
            rates = jnp.where(pore, 0.0, jnp.where(active, 0.3, 0.02))
            pairs = [around(state, f, t, ghosts) for f in range(3)]
            c, e, s = (p[0] for p in pairs)
            eta = s - e - 0.5 * c
            forward = jnp.exp(0.5 * eta)
            backward = jnp.exp(-0.5 * eta)
            current = rates * (forward - backward)
            slope = 0.5 * rates * (forward + backward)
            react = (-0.5 * current, -current, current)
            for f in range(3):
                v, total = pairs[f]
                misfit = mask * (0.5 * v + conduct[f] * (6.0 * v - total) + react[f] - source[f, t])
                square = square + misfit * misfit
                dg = 0.5 + 6.0 * conduct[f] + (0.25 * slope if f == 0 else slope)
                w = (OMEGA * mask) / dg
                b = -w * misfit
                base[f, t] = b
                upd[0, f, t, PAD:PAD + E] = b
                gain[f, t] = w * conduct[f]
                mix[f, t] = w * slope * (0.5 if f == 0 else 1.0)
                diag[f, t] = dg * (1.0 / OMEGA)
                pack_z(planes, f, t, b)
                if t == 0:
                    ends[f][0] = b
                if t == TILES - 1:
                    ends[f][1] = b
        post_y(r0 + 1, ends)
        post_z(r0 + 1, planes)
        squares_a[k, 0] = fold(square)
        gather_start(over_a, k, "space", me_s, n)

        def terms(u, t, ghosts):
            pairs = [around(u, f, t, ghosts) for f in range(3)]
            c, e, s = (p[0] for p in pairs)
            half = 0.5 * c
            cross = (s - e, s - half, e + half)
            return [(pairs[f][0], base[f, t] + gain[f, t] * pairs[f][1] + mix[f, t] * cross[f]) for f in range(3)]

        def smooth(p, carry):
            now = lax.rem(p, 2)
            u, later = upd.at[now], upd.at[1 - now]
            planes_in = ghosts_z(r0 + 1 + p, False)
            ghosts = (planes_in, (None, None))
            planes, ends = [None, None], [[None, None] for _ in range(3)]
            for t in inside + outside:
                if t == 0:
                    ghosts = (planes_in, ghosts_y(r0 + 1 + p, False))
                for f, (v, term) in enumerate(terms(u, t, ghosts)):
                    value = (1.0 - OMEGA) * v + term
                    later[f, t, PAD:PAD + E] = value
                    pack_z(planes, f, t, value)
                    if t == 0:
                        ends[f][0] = value
                    if t == TILES - 1:
                        ends[f][1] = value
            post_y(r0 + 2 + p, ends)
            post_z(r0 + 2 + p, planes)
            return carry

        lax.fori_loop(0, 1, smooth, 0)
        gather_wait(over_a, k, "space", me_s, n)
        part = squares_a[k, 0]
        for d in range(1, n):
            part = part + squares_a[k, d]
        squares_b[k, 0] = part
        gather_start(over_b, k, "group", me_g, m)
        lax.fori_loop(1, SMOOTH - 1, smooth, 0)

        u = upd.at[(SMOOTH - 1) % 2]
        planes_in = ghosts_z(r0 + SMOOTH, False)
        ghosts = (planes_in, (None, None))
        sums = [jnp.zeros((E, 128), F32) for _ in range(3)]
        for t in inside + outside:
            if t == 0:
                ghosts = (planes_in, ghosts_y(r0 + SMOOTH, False))
            for f, (v, term) in enumerate(terms(u, t, ghosts)):
                sums[f] = sums[f] + diag[f, t] * (term - OMEGA * v)
        rows = [jnp.sum(x, axis=0, keepdims=True) for x in sums]
        coarse[k, 0] = jnp.where(rows8 == 0, rows[0], jnp.where(rows8 == 1, rows[1], jnp.where(rows8 == 2, rows[2], 0.0)))
        gather_start(over_c, k, "space", me_s, n)

        gather_wait(over_b, k, "group", me_g, m)
        part = squares_b[k, 0]
        for d in range(1, m):
            part = part + squares_b[k, d]
        whole = jnp.sum(jnp.sum(part, axis=0, keepdims=True), axis=1, keepdims=True)
        cells = 3.0 * n * m * E * E * E
        damping = 1.0 / (1.0 + jnp.sqrt(whole / cells + 1e-6))

        gather_wait(over_c, k, "space", me_s, n)
        got = [coarse[k, d] for d in range(n)]
        planes, ends = [None, None], [[None, None] for _ in range(3)]
        for f in range(3):
            acc = got[0] * weights[f, 0]
            for d in range(1, n):
                acc = acc + got[d] * weights[f, d]
            lift = mask * jnp.sum(jnp.sum(acc, axis=0, keepdims=True), axis=1, keepdims=True)
            for t in range(TILES):
                value = state[f, t, PAD:PAD + E] + damping * (u[f, t, PAD:PAD + E] + lift)
                state[f, t, PAD:PAD + E] = value
                pack_z(planes, f, t, value)
                if t == 0:
                    ends[f][0] = value
                if t == TILES - 1:
                    ends[f][1] = value

        @pl.when(k < NEWTON - 1)
        def _():
            post_y(r0 + ROUNDS, ends)
            post_z(r0 + ROUNDS, planes)

        return carry

    lax.fori_loop(0, NEWTON, sweep, 0)

    for f in range(3):
        for h in range(2):
            got = swap4([state[f, 4 * h + r, PAD:PAD + E] for r in range(4)])
            for k in range(4):
                t = 2 * k + h
                out[f, :, t * 128:(t + 1) * 128] = got[k]

    for r in range(NEWTON * ROUNDS):
        for d in range(4):
            @pl.when(has(*targets[d]))
            def _():
                face_copy(r, d).wait_send()
    for k in range(NEWTON):
        for bufs, axis, me, size in ((over_a, "space", me_s, n), (over_b, "group", me_g, m), (over_c, "space", me_s, n)):
            for d in range(1, size):
                gather_copy(*bufs, k, d, axis, me, size).wait_send()


def shards(n, m, initial_state, phases, brick_coords, neighbours, source, coarse_inverse):
    rounds = NEWTON * ROUNDS
    anywhere = pl.BlockSpec(memory_space=pl.ANY)
    vmem = pl.BlockSpec(memory_space=pltpu.VMEM)
    padded = (3, TILES, E + 2 * PAD, 128)
    inner = (3, TILES, E, 128)
    dma = pltpu.SemaphoreType.DMA
    result = pl.pallas_call(
        functools.partial(kernel, n, m),
        out_shape=jax.ShapeDtypeStruct((3, E, E * E), F32),
        in_specs=[anywhere] * 6,
        out_specs=vmem,
        scratch_shapes=[
            pltpu.SMEM((1, 3), jnp.int32),
            pltpu.SMEM((1, 6), jnp.int32),
            pltpu.SMEM((3, 1, 3 * n), F32),
            pltpu.VMEM((3, E, E * E), F32),
            pltpu.VMEM((E, E * E), jnp.int32),
            pltpu.VMEM((3, E, E * E), F32),
            dma((6,)),
            pltpu.VMEM(padded, F32),
            pltpu.VMEM((2,) + padded, F32),
            pltpu.VMEM(inner, F32),
            pltpu.VMEM(inner, F32),
            pltpu.VMEM(inner, F32),
            pltpu.VMEM(inner, F32),
            pltpu.VMEM(inner, F32),
            pltpu.VMEM(inner[1:], jnp.int32),
            pltpu.VMEM((rounds, 4, E, 128), F32),
            pltpu.VMEM((rounds, 4, E, 128), F32),
            pltpu.VMEM((NEWTON, n, 8, 128), F32),
            pltpu.VMEM((NEWTON, m, 8, 128), F32),
            pltpu.VMEM((NEWTON, n, 8, 128), F32),
            pltpu.VMEM((3, n, 8, 128), F32),
            dma((rounds, 4)), dma((rounds, 4)),
            dma((NEWTON, n)), dma((NEWTON, n)),
            dma((NEWTON, m)), dma((NEWTON, m)),
            dma((NEWTON, n)), dma((NEWTON, n)),
        ],
        compiler_params=pltpu.CompilerParams(
            collective_id=0, has_side_effects=True, vmem_limit_bytes=56 * 1024 * 1024
        ),
    )(brick_coords, neighbours, jnp.swapaxes(coarse_inverse, 0, 1), initial_state[0], phases[0], source[0])
    return result[None]


def solution(mesh):
    both = ("group", "space")
    return jax.shard_map(
        functools.partial(shards, mesh.shape["space"], mesh.shape["group"]),
        mesh=mesh,
        in_specs=(
            P(both, None, None, None),
            P(both, None, None),
            P(both, None),
            P(both, None),
            P(both, None, None, None),
            P("group", "space", None),
        ),
        out_specs=P(both, None, None, None),
        check_vma=False,
    )
```

```python
import functools

import jax
import jax.numpy as jnp
from jax import lax
from jax.experimental import pallas as pl
from jax.experimental.pallas import tpu as pltpu
from jax.sharding import PartitionSpec as P

NEWTON = 2
SMOOTH = 4
ROUNDS = SMOOTH + 1
E = 32
TILES = 8
PAD = 8
OMEGA = 0.8
MESH = pl.DeviceIdType.MESH
F32 = jnp.float32


def roll(x, shift):
    shift = shift % 128
    return x if shift == 0 else pltpu.roll(x, shift, 1)


def place(f, t):
    return (0, 16 * f + 2 * t) if f < 2 else (1, 2 * t)


def kernel(
    n, m,
    coords_in, links_in, inverse_in, state_hbm, phase_hbm, source_hbm, out,
    coords, links, inverse, state_in, phase_in, source_in, fetch,
    state, upd, base, gain, mix, diag, source, phase,
    send, recv, squares_a, squares_b, coarse, weights,
    face_send, face_recv, a_send, a_recv, b_send, b_recv, c_send, c_recv,
):
    me_s = lax.axis_index("space")
    me_g = lax.axis_index("group")
    lane = lax.broadcasted_iota(jnp.int32, (E, 128), 1)
    block = lane // 32
    depth = lane % 32
    first = depth == 0
    last = depth == 31
    edge = first | last
    even = lane % 2 == 0

    fetches = [
        pltpu.make_async_copy(a, b, fetch.at[i])
        for i, (a, b) in enumerate((
            (state_hbm, state_in), (coords_in, coords), (links_in, links),
            (phase_hbm, phase_in), (source_hbm, source_in), (inverse_in, inverse),
        ))
    ]
    for copy in fetches:
        copy.start()

    targets = (("space", me_s, 1, n), ("space", me_s, -1, n), ("group", me_g, 1, m), ("group", me_g, -1, m))

    def has(axis, me, step, size):
        return me + step < size if step > 0 else me + step >= 0

    barrier = pltpu.get_barrier_semaphore()
    for axis, me, size in (("space", me_s, n), ("group", me_g, m)):
        for d in range(1, size):
            pl.semaphore_signal(barrier, inc=1, device_id={axis: lax.rem(me + d, size)}, device_id_type=MESH)

    def face_copy(r, d):
        axis, me, step, size = targets[d]
        return pltpu.make_async_remote_copy(
            src_ref=send.at[r, d], dst_ref=recv.at[r, d],
            send_sem=face_send.at[r, d], recv_sem=face_recv.at[r, d],
            device_id={axis: jnp.clip(me + step, 0, size - 1)}, device_id_type=MESH)

    def source_of(d):
        axis, me, step, size = targets[d]
        return has(axis, me, -step, size)

    def start_faces(r, which):
        for d in which:
            @pl.when(has(*targets[d]))
            def _():
                face_copy(r, d).start()

    def wait_faces(r, which):
        for d in which:
            @pl.when(source_of(d))
            def _():
                face_copy(r, d).wait_recv()

    def gather_copy(buf, ss, rs, k, d, axis, me, size):
        return pltpu.make_async_remote_copy(
            src_ref=buf.at[k, 0], dst_ref=buf.at[k, d],
            send_sem=ss.at[k, d], recv_sem=rs.at[k, d],
            device_id={axis: lax.rem(me + d, size)}, device_id_type=MESH)

    over_a = (squares_a, a_send, a_recv)
    over_b = (squares_b, b_send, b_recv)
    over_c = (coarse, c_send, c_recv)

    def gather_start(bufs, k, axis, me, size):
        for d in range(1, size):
            gather_copy(*bufs, k, d, axis, me, size).start()

    def gather_wait(bufs, k, axis, me, size):
        for d in range(1, size):
            gather_copy(*bufs, k, d, axis, me, size).wait_recv()


    def swap4(a):
        low = block < 2
        t0 = jnp.where(low, a[0], roll(a[2], 64))
        t2 = jnp.where(low, roll(a[0], 64), a[2])
        t1 = jnp.where(low, a[1], roll(a[3], 64))
        t3 = jnp.where(low, roll(a[1], 64), a[3])
        ev = block % 2 == 0
        return (jnp.where(ev, t0, roll(t1, 32)), jnp.where(ev, roll(t0, 96), t1),
                jnp.where(ev, t2, roll(t3, 32)), jnp.where(ev, roll(t2, 96), t3))

    def spread_in(load):
        tiles = [None] * 8
        for h in range(2):
            got = swap4([load(2 * k + h) for k in range(4)])
            for r in range(4):
                tiles[4 * h + r] = got[r]
        return tiles

    fetches[1].wait()
    fetches[2].wait()
    occupied = coords[0, 0] >= 0
    mask = jnp.where(occupied, 1.0, 0.0).astype(F32)
    wall = coords[0, 0].astype(F32) + coords[0, 1].astype(F32) / n + coords[0, 2].astype(F32) / m - 1.0
    linked = [links[0, 2 + d] >= 0 for d in range(4)]

    zero_rows = jnp.zeros((PAD, 128), F32)
    for f in range(3):
        for t in range(TILES):
            edge_rows = zero_rows if f < 2 else zero_rows + wall
            state[f, t, 0:PAD] = edge_rows
            state[f, t, PAD + E:] = edge_rows
            for b in range(2):
                upd[b, f, t, 0:PAD] = zero_rows
                upd[b, f, t, PAD + E:] = zero_rows
    fetches[0].wait()
    for f in range(3):
        tiles = spread_in(lambda t: state_in[f, :, t * 128:(t + 1) * 128])
        for t in range(TILES):
            state[f, t, PAD:PAD + E] = tiles[t] * mask

    def pack_z(planes, f, t, c):
        q, j = place(f, t)
        part = roll(jnp.where(edge, c, 0.0), j)
        planes[q] = part if planes[q] is None else planes[q] + part

    def y_planes(ends):
        up = jnp.where(block == 0, roll(ends[0][1], -96), jnp.where(block == 1, roll(ends[1][1], -64), roll(ends[2][1], -32)))
        down = jnp.where(block == 0, ends[0][0], jnp.where(block == 1, roll(ends[1][0], 32), roll(ends[2][0], 64)))
        return [up, down]

    def z_planes(planes):
        q0, q1 = planes
        return [jnp.where(even, roll(q1, -1), q0), jnp.where(even, q0, roll(q1, 1))]

    def post_y(r, ends):
        send[r, 0], send[r, 1] = y_planes(ends)
        start_faces(r, (0, 1))

    def post_z(r, planes):
        send[r, 2], send[r, 3] = z_planes(planes)
        start_faces(r, (2, 3))

    def walled(r, d, walls):
        got = recv[r, d]
        if not walls:
            return got, got
        return jnp.where(linked[d], got, 0.0), jnp.where(linked[d], got, wall)

    def ghosts_z(r, walls):
        wait_faces(r, (2, 3))
        low, solid_low = walled(r, 2, walls)
        high, solid_high = walled(r, 3, walls)
        c0 = jnp.where(even, high, roll(low, 66))
        c1 = jnp.where(even, roll(solid_high, -1), roll(solid_low, 67))
        return c0, c1

    def ghosts_y(r, walls):
        wait_faces(r, (0, 1))
        low = walled(r, 0, walls)
        high = walled(r, 1, walls)
        lows = [roll(low[f // 2], -32 * f) for f in range(3)]
        highs = [roll(high[f // 2], 96 - 32 * f) for f in range(3)]
        return lows, highs

    inside = tuple(range(1, TILES - 1))
    outside = (0, TILES - 1)

    def around(ref, f, t, ghosts):
        planes, (lows, highs) = ghosts
        c = ref[f, t, PAD:PAD + E]
        total = ref[f, t, PAD - 1:PAD - 1 + E] + ref[f, t, PAD + 1:PAD + 1 + E]
        if t > 0:
            total = total + ref[f, t - 1, PAD:PAD + E]
        else:
            total = total + jnp.where(block == 0, lows[f], roll(ref[f, TILES - 1, PAD:PAD + E], 32))
        if t < TILES - 1:
            total = total + ref[f, t + 1, PAD:PAD + E]
        else:
            total = total + jnp.where(block == 3, highs[f], roll(ref[f, 0, PAD:PAD + E], -32))
        q, j = place(f, t)
        ghost = roll(planes[q], 31 - j)
        total = total + jnp.where(last, ghost, roll(c, -1)) + jnp.where(first, ghost, roll(c, 1))
        return c, total

    def pack_state():
        planes, ends = [None, None], []
        for f in range(3):
            tiles = [state[f, t, PAD:PAD + E] for t in range(TILES)]
            for t in range(TILES):
                pack_z(planes, f, t, tiles[t])
            ends.append((tiles[0], tiles[TILES - 1]))
        return planes, ends

    planes, ends = pack_state()
    pl.semaphore_wait(barrier, n + m - 2)
    post_y(0, ends)
    post_z(0, planes)

    rows8 = lax.broadcasted_iota(jnp.int32, (8, 128), 0)
    blank = jnp.zeros((E, 128), F32)
    for d in range(4):
        @pl.when(jnp.logical_not(source_of(d)))
        def _():
            for r in range(NEWTON * ROUNDS):
                recv[r, d] = blank
    for copy in fetches[3:]:
        copy.wait()
    for f in range(3):
        tiles = spread_in(lambda t: source_in[f, :, t * 128:(t + 1) * 128])
        for t in range(TILES):
            source[f, t] = tiles[t]
    tiles = spread_in(lambda t: phase_in[:, t * 128:(t + 1) * 128])
    for t in range(TILES):
        phase[t] = tiles[t]
    for d in range(n):
        owner = lax.rem(me_s - d + n, n)
        for i in range(3):
            v = [inverse[i, 0, 3 * owner + f] for f in range(3)]
            weights[i, d] = jnp.where(rows8 == 0, v[0], jnp.where(rows8 == 1, v[1], jnp.where(rows8 == 2, v[2], 0.0)))

    def fold(x):
        return x[0:8] + x[8:16] + x[16:24] + x[24:32]

    def sweep(k, carry):
        r0 = k * ROUNDS
        planes_in = ghosts_z(r0, True)
        ghosts = (planes_in, (None, None))
        planes, ends = [None, None], [[None, None] for _ in range(3)]
        square = jnp.zeros((E, 128), F32)
        for t in inside + outside:
            if t == 0:
                ghosts = (planes_in, ghosts_y(r0, True))
            label = phase[t]
            pore = label == 0
            active = label == 1
            conduct = (jnp.where(pore, 1.0, 0.2), jnp.where(pore, 1.0, 0.1),
                       jnp.where(pore, 0.05, jnp.where(active, 0.5, 1.5)))
            rates = jnp.where(pore, 0.0, jnp.where(active, 0.3, 0.02))
            pairs = [around(state, f, t, ghosts) for f in range(3)]
            c, e, s = (p[0] for p in pairs)
            eta = s - e - 0.5 * c
            forward = jnp.exp(0.5 * eta)
            backward = jnp.exp(-0.5 * eta)
            current = rates * (forward - backward)
            slope = 0.5 * rates * (forward + backward)
            react = (-0.5 * current, -current, current)
            for f in range(3):
                v, total = pairs[f]
                misfit = mask * (0.5 * v + conduct[f] * (6.0 * v - total) + react[f] - source[f, t])
                square = square + misfit * misfit
                dg = 0.5 + 6.0 * conduct[f] + (0.25 * slope if f == 0 else slope)
                w = (OMEGA * mask) / dg
                b = -w * misfit
                base[f, t] = b
                upd[0, f, t, PAD:PAD + E] = b
                gain[f, t] = w * conduct[f]
                mix[f, t] = w * slope * (0.5 if f == 0 else 1.0)
                diag[f, t] = dg * (1.0 / OMEGA)
                pack_z(planes, f, t, b)
                if t == 0:
                    ends[f][0] = b
                if t == TILES - 1:
                    ends[f][1] = b
        post_y(r0 + 1, ends)
        post_z(r0 + 1, planes)
        squares_a[k, 0] = fold(square)
        gather_start(over_a, k, "space", me_s, n)

        def terms(u, t, ghosts):
            pairs = [around(u, f, t, ghosts) for f in range(3)]
            c, e, s = (p[0] for p in pairs)
            half = 0.5 * c
            cross = (s - e, s - half, e + half)
            return [(pairs[f][0], base[f, t] + gain[f, t] * pairs[f][1] + mix[f, t] * cross[f]) for f in range(3)]

        def smooth(p, carry):
            now = lax.rem(p, 2)
            u, later = upd.at[now], upd.at[1 - now]
            planes_in = ghosts_z(r0 + 1 + p, False)
            ghosts = (planes_in, (None, None))
            planes, ends = [None, None], [[None, None] for _ in range(3)]
            for t in inside + outside:
                if t == 0:
                    ghosts = (planes_in, ghosts_y(r0 + 1 + p, False))
                for f, (v, term) in enumerate(terms(u, t, ghosts)):
                    value = (1.0 - OMEGA) * v + term
                    later[f, t, PAD:PAD + E] = value
                    pack_z(planes, f, t, value)
                    if t == 0:
                        ends[f][0] = value
                    if t == TILES - 1:
                        ends[f][1] = value
            post_y(r0 + 2 + p, ends)
            post_z(r0 + 2 + p, planes)
            return carry

        lax.fori_loop(0, 1, smooth, 0)
        gather_wait(over_a, k, "space", me_s, n)
        part = squares_a[k, 0]
        for d in range(1, n):
            part = part + squares_a[k, d]
        squares_b[k, 0] = part
        gather_start(over_b, k, "group", me_g, m)
        lax.fori_loop(1, SMOOTH - 1, smooth, 0)

        u = upd.at[(SMOOTH - 1) % 2]
        planes_in = ghosts_z(r0 + SMOOTH, False)
        ghosts = (planes_in, (None, None))
        sums = [jnp.zeros((E, 128), F32) for _ in range(3)]
        for t in inside + outside:
            if t == 0:
                ghosts = (planes_in, ghosts_y(r0 + SMOOTH, False))
            for f, (v, term) in enumerate(terms(u, t, ghosts)):
                sums[f] = sums[f] + diag[f, t] * (term - OMEGA * v)
        rows = [jnp.sum(x, axis=0, keepdims=True) for x in sums]
        coarse[k, 0] = jnp.where(rows8 == 0, rows[0], jnp.where(rows8 == 1, rows[1], jnp.where(rows8 == 2, rows[2], 0.0)))
        gather_start(over_c, k, "space", me_s, n)

        gather_wait(over_b, k, "group", me_g, m)
        part = squares_b[k, 0]
        for d in range(1, m):
            part = part + squares_b[k, d]
        whole = jnp.sum(jnp.sum(part, axis=0, keepdims=True), axis=1, keepdims=True)
        cells = 3.0 * n * m * E * E * E
        damping = 1.0 / (1.0 + jnp.sqrt(whole / cells + 1e-6))

        planes, ends = [None, None], []
        for f in range(3):
            tiles = []
            for t in range(TILES):
                value = state[f, t, PAD:PAD + E] + damping * u[f, t, PAD:PAD + E]
                state[f, t, PAD:PAD + E] = value
                pack_z(planes, f, t, value)
                tiles.append(value)
            ends.append((tiles[0], tiles[TILES - 1]))
            for h in range(2):
                got = swap4(tiles[4 * h:4 * h + 4])
                for q in range(4):
                    t = 2 * q + h
                    out[f, :, t * 128:(t + 1) * 128] = got[q]
        pack = y_planes(ends) + z_planes(planes)

        gather_wait(over_c, k, "space", me_s, n)
        got = [coarse[k, d] for d in range(n)]
        lifts = []
        for f in range(3):
            acc = got[0] * weights[f, 0]
            for d in range(1, n):
                acc = acc + got[d] * weights[f, d]
            lifts.append(damping * (mask * jnp.sum(jnp.sum(acc, axis=0, keepdims=True), axis=1, keepdims=True)))

        @pl.when(k < NEWTON - 1)
        def _():
            by_block = jnp.where(block == 0, lifts[0], jnp.where(block == 1, lifts[1], lifts[2]))
            below = jnp.where(even, lifts[2], jnp.where((depth < 15) | last, lifts[0], lifts[1]))
            above = jnp.where(even, jnp.where(depth < 16, lifts[0], lifts[1]), lifts[2])
            for d, part in enumerate((by_block, by_block, below, above)):
                send[r0 + ROUNDS, d] = pack[d] + part
            start_faces(r0 + ROUNDS, (0, 1, 2, 3))
            for f in range(3):
                for t in range(TILES):
                    state[f, t, PAD:PAD + E] = state[f, t, PAD:PAD + E] + lifts[f]

        @pl.when(k == NEWTON - 1)
        def _():
            for f in range(3):
                out[f] = out[f] + lifts[f]

        return carry

    lax.fori_loop(0, NEWTON, sweep, 0)

    for r in range(NEWTON * ROUNDS):
        for d in range(4):
            @pl.when(has(*targets[d]))
            def _():
                face_copy(r, d).wait_send()
    for k in range(NEWTON):
        for bufs, axis, me, size in ((over_a, "space", me_s, n), (over_b, "group", me_g, m), (over_c, "space", me_s, n)):
            for d in range(1, size):
                gather_copy(*bufs, k, d, axis, me, size).wait_send()


def shards(n, m, initial_state, phases, brick_coords, neighbours, source, coarse_inverse):
    rounds = NEWTON * ROUNDS
    anywhere = pl.BlockSpec(memory_space=pl.ANY)
    vmem = pl.BlockSpec(memory_space=pltpu.VMEM)
    padded = (3, TILES, E + 2 * PAD, 128)
    inner = (3, TILES, E, 128)
    dma = pltpu.SemaphoreType.DMA
    result = pl.pallas_call(
        functools.partial(kernel, n, m),
        out_shape=jax.ShapeDtypeStruct((3, E, E * E), F32),
        in_specs=[anywhere] * 6,
        out_specs=vmem,
        scratch_shapes=[
            pltpu.SMEM((1, 3), jnp.int32),
            pltpu.SMEM((1, 6), jnp.int32),
            pltpu.SMEM((3, 1, 3 * n), F32),
            pltpu.VMEM((3, E, E * E), F32),
            pltpu.VMEM((E, E * E), jnp.int32),
            pltpu.VMEM((3, E, E * E), F32),
            dma((6,)),
            pltpu.VMEM(padded, F32),
            pltpu.VMEM((2,) + padded, F32),
            pltpu.VMEM(inner, F32),
            pltpu.VMEM(inner, F32),
            pltpu.VMEM(inner, F32),
            pltpu.VMEM(inner, F32),
            pltpu.VMEM(inner, F32),
            pltpu.VMEM(inner[1:], jnp.int32),
            pltpu.VMEM((rounds, 4, E, 128), F32),
            pltpu.VMEM((rounds, 4, E, 128), F32),
            pltpu.VMEM((NEWTON, n, 8, 128), F32),
            pltpu.VMEM((NEWTON, m, 8, 128), F32),
            pltpu.VMEM((NEWTON, n, 8, 128), F32),
            pltpu.VMEM((3, n, 8, 128), F32),
            dma((rounds, 4)), dma((rounds, 4)),
            dma((NEWTON, n)), dma((NEWTON, n)),
            dma((NEWTON, m)), dma((NEWTON, m)),
            dma((NEWTON, n)), dma((NEWTON, n)),
        ],
        compiler_params=pltpu.CompilerParams(
            collective_id=0, has_side_effects=True, vmem_limit_bytes=56 * 1024 * 1024
        ),
    )(brick_coords, neighbours, jnp.swapaxes(coarse_inverse, 0, 1), initial_state[0], phases[0], source[0])
    return result[None]


def solution(mesh):
    both = ("group", "space")
    return jax.shard_map(
        functools.partial(shards, mesh.shape["space"], mesh.shape["group"]),
        mesh=mesh,
        in_specs=(
            P(both, None, None, None),
            P(both, None, None),
            P(both, None),
            P(both, None),
            P(both, None, None, None),
            P("group", "space", None),
        ),
        out_specs=P(both, None, None, None),
        check_vma=False,
    )
```

```python
import functools

import jax
import jax.numpy as jnp
from jax import lax
from jax.experimental import pallas as pl
from jax.experimental.pallas import tpu as pltpu
from jax.sharding import PartitionSpec as P

NEWTON = 2
SMOOTH = 4
ROUNDS = SMOOTH + 1
E = 32
TILES = 8
PAD = 8
OMEGA = 0.8
MESH = pl.DeviceIdType.MESH
F32 = jnp.float32


def roll(x, shift):
    shift = shift % 128
    return x if shift == 0 else pltpu.roll(x, shift, 1)


def place(f, t):
    return (0, 16 * f + 2 * t) if f < 2 else (1, 2 * t)


def kernel(
    n, m,
    coords_in, links_in, inverse_in, state_hbm, phase_hbm, source_hbm, out,
    coords, links, inverse, state_in, phase_in, source_in, fetch,
    state, upd, base, gain, mix, diag, source, phase,
    send, recv, squares_a, squares_b, coarse, weights,
    face_send, face_recv, a_send, a_recv, b_send, b_recv, c_send, c_recv,
):
    me_s = lax.axis_index("space")
    me_g = lax.axis_index("group")
    lane = lax.broadcasted_iota(jnp.int32, (E, 128), 1)
    block = lane // 32
    depth = lane % 32
    first = depth == 0
    last = depth == 31
    edge = first | last
    even = lane % 2 == 0

    fetches = [
        pltpu.make_async_copy(a, b, fetch.at[i])
        for i, (a, b) in enumerate((
            (state_hbm, state_in), (coords_in, coords), (links_in, links),
            (phase_hbm, phase_in), (source_hbm, source_in), (inverse_in, inverse),
        ))
    ]
    for copy in fetches:
        copy.start()

    targets = (("space", me_s, 1, n), ("space", me_s, -1, n), ("group", me_g, 1, m), ("group", me_g, -1, m))

    def has(axis, me, step, size):
        return me + step < size if step > 0 else me + step >= 0

    barrier = pltpu.get_barrier_semaphore()
    for axis, me, size in (("space", me_s, n), ("group", me_g, m)):
        for d in range(1, size):
            pl.semaphore_signal(barrier, inc=1, device_id={axis: lax.rem(me + d, size)}, device_id_type=MESH)

    def face_copy(r, d):
        axis, me, step, size = targets[d]
        return pltpu.make_async_remote_copy(
            src_ref=send.at[r, d], dst_ref=recv.at[r, d],
            send_sem=face_send.at[r, d], recv_sem=face_recv.at[r, d],
            device_id={axis: jnp.clip(me + step, 0, size - 1)}, device_id_type=MESH)

    def source_of(d):
        axis, me, step, size = targets[d]
        return has(axis, me, -step, size)

    def start_faces(r, which):
        for d in which:
            @pl.when(has(*targets[d]))
            def _():
                face_copy(r, d).start()

    def wait_faces(r, which):
        for d in which:
            @pl.when(source_of(d))
            def _():
                face_copy(r, d).wait_recv()

    def gather_copy(buf, ss, rs, k, d, axis, me, size):
        return pltpu.make_async_remote_copy(
            src_ref=buf.at[k, 0], dst_ref=buf.at[k, d],
            send_sem=ss.at[k, d], recv_sem=rs.at[k, d],
            device_id={axis: lax.rem(me + d, size)}, device_id_type=MESH)

    over_a = (squares_a, a_send, a_recv)
    over_b = (squares_b, b_send, b_recv)
    over_c = (coarse, c_send, c_recv)

    def gather_start(bufs, k, axis, me, size):
        for d in range(1, size):
            gather_copy(*bufs, k, d, axis, me, size).start()

    def gather_wait(bufs, k, axis, me, size):
        for d in range(1, size):
            gather_copy(*bufs, k, d, axis, me, size).wait_recv()


    def swap4(a):
        low = block < 2
        t0 = jnp.where(low, a[0], roll(a[2], 64))
        t2 = jnp.where(low, roll(a[0], 64), a[2])
        t1 = jnp.where(low, a[1], roll(a[3], 64))
        t3 = jnp.where(low, roll(a[1], 64), a[3])
        ev = block % 2 == 0
        return (jnp.where(ev, t0, roll(t1, 32)), jnp.where(ev, roll(t0, 96), t1),
                jnp.where(ev, t2, roll(t3, 32)), jnp.where(ev, roll(t2, 96), t3))

    def spread_in(load):
        tiles = [None] * 8
        for h in range(2):
            got = swap4([load(2 * k + h) for k in range(4)])
            for r in range(4):
                tiles[4 * h + r] = got[r]
        return tiles

    fetches[1].wait()
    fetches[2].wait()
    occupied = coords[0, 0] >= 0
    mask = jnp.where(occupied, 1.0, 0.0).astype(F32)
    wall = coords[0, 0].astype(F32) + coords[0, 1].astype(F32) / n + coords[0, 2].astype(F32) / m - 1.0
    linked = [links[0, 2 + d] >= 0 for d in range(4)]

    zero_rows = jnp.zeros((PAD, 128), F32)
    for f in range(3):
        for t in range(TILES):
            edge_rows = zero_rows if f < 2 else zero_rows + wall
            state[f, t, 0:PAD] = edge_rows
            state[f, t, PAD + E:] = edge_rows
            for b in range(2):
                upd[b, f, t, 0:PAD] = zero_rows
                upd[b, f, t, PAD + E:] = zero_rows
    fetches[0].wait()
    for f in range(3):
        tiles = spread_in(lambda t: state_in[f, :, t * 128:(t + 1) * 128])
        for t in range(TILES):
            state[f, t, PAD:PAD + E] = tiles[t] * mask

    def pack_z(planes, f, t, c):
        q, j = place(f, t)
        part = roll(jnp.where(edge, c, 0.0), j)
        planes[q] = part if planes[q] is None else planes[q] + part

    def y_planes(ends):
        up = jnp.where(block == 0, roll(ends[0][1], -96), jnp.where(block == 1, roll(ends[1][1], -64), roll(ends[2][1], -32)))
        down = jnp.where(block == 0, ends[0][0], jnp.where(block == 1, roll(ends[1][0], 32), roll(ends[2][0], 64)))
        return [up, down]

    def z_planes(planes):
        q0, q1 = planes
        return [jnp.where(even, roll(q1, -1), q0), jnp.where(even, q0, roll(q1, 1))]

    def post_y(r, ends):
        send[r, 0], send[r, 1] = y_planes(ends)
        start_faces(r, (0, 1))

    def post_z(r, planes):
        send[r, 2], send[r, 3] = z_planes(planes)
        start_faces(r, (2, 3))

    def walled(r, d, walls):
        got = recv[r, d]
        if not walls:
            return got, got
        return jnp.where(linked[d], got, 0.0), jnp.where(linked[d], got, wall)

    def ghosts_z(r, walls):
        wait_faces(r, (2, 3))
        low, solid_low = walled(r, 2, walls)
        high, solid_high = walled(r, 3, walls)
        c0 = jnp.where(even, high, roll(low, 66))
        c1 = jnp.where(even, roll(solid_high, -1), roll(solid_low, 67))
        return c0, c1

    def ghosts_y(r, walls):
        wait_faces(r, (0, 1))
        low = walled(r, 0, walls)
        high = walled(r, 1, walls)
        lows = [roll(low[f // 2], -32 * f) for f in range(3)]
        highs = [roll(high[f // 2], 96 - 32 * f) for f in range(3)]
        return lows, highs

    inside = tuple(range(1, TILES - 1))
    outside = (0, TILES - 1)

    def around(ref, f, t, ghosts):
        planes, (lows, highs) = ghosts
        c = ref[f, t, PAD:PAD + E]
        total = ref[f, t, PAD - 1:PAD - 1 + E] + ref[f, t, PAD + 1:PAD + 1 + E]
        if t > 0:
            total = total + ref[f, t - 1, PAD:PAD + E]
        else:
            total = total + jnp.where(block == 0, lows[f], roll(ref[f, TILES - 1, PAD:PAD + E], 32))
        if t < TILES - 1:
            total = total + ref[f, t + 1, PAD:PAD + E]
        else:
            total = total + jnp.where(block == 3, highs[f], roll(ref[f, 0, PAD:PAD + E], -32))
        q, j = place(f, t)
        ghost = roll(planes[q], 31 - j)
        total = total + jnp.where(last, ghost, roll(c, -1)) + jnp.where(first, ghost, roll(c, 1))
        return c, total

    def pack_state():
        planes, ends = [None, None], []
        for f in range(3):
            tiles = [state[f, t, PAD:PAD + E] for t in range(TILES)]
            for t in range(TILES):
                pack_z(planes, f, t, tiles[t])
            ends.append((tiles[0], tiles[TILES - 1]))
        return planes, ends

    planes, ends = pack_state()
    pl.semaphore_wait(barrier, n + m - 2)
    post_y(0, ends)
    post_z(0, planes)

    rows8 = lax.broadcasted_iota(jnp.int32, (8, 128), 0)
    blank = jnp.zeros((E, 128), F32)
    for d in range(4):
        @pl.when(jnp.logical_not(source_of(d)))
        def _():
            for r in range(NEWTON * ROUNDS):
                recv[r, d] = blank
    for copy in fetches[3:]:
        copy.wait()
    for f in range(3):
        tiles = spread_in(lambda t: source_in[f, :, t * 128:(t + 1) * 128])
        for t in range(TILES):
            source[f, t] = tiles[t]
    tiles = spread_in(lambda t: phase_in[:, t * 128:(t + 1) * 128])
    for t in range(TILES):
        phase[t] = tiles[t]
    for d in range(n):
        owner = lax.rem(me_s - d + n, n)
        for i in range(3):
            v = [inverse[i, 0, 3 * owner + f] for f in range(3)]
            weights[i, d] = jnp.where(rows8 == 0, v[0], jnp.where(rows8 == 1, v[1], jnp.where(rows8 == 2, v[2], 0.0)))

    def fold(x):
        return x[0:8] + x[8:16] + x[16:24] + x[24:32]

    def sweep(k, carry):
        r0 = k * ROUNDS
        planes_in = ghosts_z(r0, True)
        ghosts = (planes_in, (None, None))
        planes, ends = [None, None], [[None, None] for _ in range(3)]
        square = jnp.zeros((E, 128), F32)
        for t in inside + outside:
            if t == 0:
                ghosts = (planes_in, ghosts_y(r0, True))
            label = phase[t]
            pore = label == 0
            active = label == 1
            conduct = (jnp.where(pore, 1.0, 0.2), jnp.where(pore, 1.0, 0.1),
                       jnp.where(pore, 0.05, jnp.where(active, 0.5, 1.5)))
            rates = jnp.where(pore, 0.0, jnp.where(active, 0.3, 0.02))
            pairs = [around(state, f, t, ghosts) for f in range(3)]
            c, e, s = (p[0] for p in pairs)
            eta = s - e - 0.5 * c
            forward = jnp.exp(0.5 * eta)
            backward = jnp.exp(-0.5 * eta)
            current = rates * (forward - backward)
            slope = 0.5 * rates * (forward + backward)
            react = (-0.5 * current, -current, current)
            for f in range(3):
                v, total = pairs[f]
                misfit = mask * (0.5 * v + conduct[f] * (6.0 * v - total) + react[f] - source[f, t])
                square = square + misfit * misfit
                dg = 0.5 + 6.0 * conduct[f] + (0.25 * slope if f == 0 else slope)
                w = (OMEGA * mask) / dg
                b = -w * misfit
                base[f, t] = b
                upd[0, f, t, PAD:PAD + E] = b
                gain[f, t] = w * conduct[f]
                mix[f, t] = w * slope * (0.5 if f == 0 else 1.0)
                diag[f, t] = dg * (1.0 / OMEGA)
                pack_z(planes, f, t, b)
                if t == 0:
                    ends[f][0] = b
                if t == TILES - 1:
                    ends[f][1] = b
        post_y(r0 + 1, ends)
        post_z(r0 + 1, planes)
        squares_a[k, 0] = fold(square)
        gather_start(over_a, k, "space", me_s, n)

        def terms(u, t, ghosts):
            pairs = [around(u, f, t, ghosts) for f in range(3)]
            c, e, s = (p[0] for p in pairs)
            half = 0.5 * c
            cross = (s - e, s - half, e + half)
            return [(pairs[f][0], base[f, t] + gain[f, t] * pairs[f][1] + mix[f, t] * cross[f]) for f in range(3)]

        no_y = ([0.0] * 3, [0.0] * 3)

        def y_extras(r):
            lows, highs = ghosts_y(r, False)
            for f in range(3):
                yield f, 0, gain[f, 0] * jnp.where(block == 0, lows[f], 0.0)
                yield f, TILES - 1, gain[f, TILES - 1] * jnp.where(block == 3, highs[f], 0.0)

        def smooth(p, carry):
            now = lax.rem(p, 2)
            u, later = upd.at[now], upd.at[1 - now]
            ghosts = (ghosts_z(r0 + 1 + p, False), no_y)
            parts = {}
            planes, ends = [None, None], [[None, None] for _ in range(3)]
            for t in inside + outside:
                for f, (v, term) in enumerate(terms(u, t, ghosts)):
                    value = (1.0 - OMEGA) * v + term
                    if t in outside:
                        parts[f, t] = value
                    else:
                        later[f, t, PAD:PAD + E] = value
                        pack_z(planes, f, t, value)
            for f, t, extra in y_extras(r0 + 1 + p):
                ends[f][t // (TILES - 1)] = parts[f, t] + extra
            post_y(r0 + 2 + p, ends)
            for f in range(3):
                for t in outside:
                    value = ends[f][t // (TILES - 1)]
                    later[f, t, PAD:PAD + E] = value
                    pack_z(planes, f, t, value)
            post_z(r0 + 2 + p, planes)
            return carry

        lax.fori_loop(0, 1, smooth, 0)
        gather_wait(over_a, k, "space", me_s, n)
        part = squares_a[k, 0]
        for d in range(1, n):
            part = part + squares_a[k, d]
        squares_b[k, 0] = part
        gather_start(over_b, k, "group", me_g, m)
        lax.fori_loop(1, SMOOTH - 1, smooth, 0)

        u = upd.at[(SMOOTH - 1) % 2]
        ghosts = (ghosts_z(r0 + SMOOTH, False), no_y)
        sums = [jnp.zeros((E, 128), F32) for _ in range(3)]
        for t in inside + outside:
            for f, (v, term) in enumerate(terms(u, t, ghosts)):
                sums[f] = sums[f] + diag[f, t] * (term - OMEGA * v)
        for f, t, extra in y_extras(r0 + SMOOTH):
            sums[f] = sums[f] + diag[f, t] * extra
        rows = [jnp.sum(x, axis=0, keepdims=True) for x in sums]
        coarse[k, 0] = jnp.where(rows8 == 0, rows[0], jnp.where(rows8 == 1, rows[1], jnp.where(rows8 == 2, rows[2], 0.0)))
        gather_start(over_c, k, "space", me_s, n)

        gather_wait(over_b, k, "group", me_g, m)
        part = squares_b[k, 0]
        for d in range(1, m):
            part = part + squares_b[k, d]
        whole = jnp.sum(jnp.sum(part, axis=0, keepdims=True), axis=1, keepdims=True)
        cells = 3.0 * n * m * E * E * E
        damping = 1.0 / (1.0 + jnp.sqrt(whole / cells + 1e-6))

        planes, ends = [None, None], []
        for f in range(3):
            tiles = []
            for t in range(TILES):
                value = state[f, t, PAD:PAD + E] + damping * u[f, t, PAD:PAD + E]
                state[f, t, PAD:PAD + E] = value
                pack_z(planes, f, t, value)
                tiles.append(value)
            ends.append((tiles[0], tiles[TILES - 1]))
            for h in range(2):
                got = swap4(tiles[4 * h:4 * h + 4])
                for q in range(4):
                    t = 2 * q + h
                    out[f, :, t * 128:(t + 1) * 128] = got[q]
        pack = y_planes(ends) + z_planes(planes)

        gather_wait(over_c, k, "space", me_s, n)
        got = [coarse[k, d] for d in range(n)]
        lifts = []
        for f in range(3):
            acc = got[0] * weights[f, 0]
            for d in range(1, n):
                acc = acc + got[d] * weights[f, d]
            lifts.append(damping * (mask * jnp.sum(jnp.sum(acc, axis=0, keepdims=True), axis=1, keepdims=True)))

        @pl.when(k < NEWTON - 1)
        def _():
            by_block = jnp.where(block == 0, lifts[0], jnp.where(block == 1, lifts[1], lifts[2]))
            below = jnp.where(even, lifts[2], jnp.where((depth < 15) | last, lifts[0], lifts[1]))
            above = jnp.where(even, jnp.where(depth < 16, lifts[0], lifts[1]), lifts[2])
            for d, part in enumerate((by_block, by_block, below, above)):
                send[r0 + ROUNDS, d] = pack[d] + part
            start_faces(r0 + ROUNDS, (0, 1, 2, 3))
            for f in range(3):
                for t in range(TILES):
                    state[f, t, PAD:PAD + E] = state[f, t, PAD:PAD + E] + lifts[f]

        @pl.when(k == NEWTON - 1)
        def _():
            for f in range(3):
                out[f] = out[f] + lifts[f]

        return carry

    lax.fori_loop(0, NEWTON, sweep, 0)

    for r in range(NEWTON * ROUNDS):
        for d in range(4):
            @pl.when(has(*targets[d]))
            def _():
                face_copy(r, d).wait_send()
    for k in range(NEWTON):
        for bufs, axis, me, size in ((over_a, "space", me_s, n), (over_b, "group", me_g, m), (over_c, "space", me_s, n)):
            for d in range(1, size):
                gather_copy(*bufs, k, d, axis, me, size).wait_send()


def shards(n, m, initial_state, phases, brick_coords, neighbours, source, coarse_inverse):
    rounds = NEWTON * ROUNDS
    anywhere = pl.BlockSpec(memory_space=pl.ANY)
    vmem = pl.BlockSpec(memory_space=pltpu.VMEM)
    padded = (3, TILES, E + 2 * PAD, 128)
    inner = (3, TILES, E, 128)
    dma = pltpu.SemaphoreType.DMA
    result = pl.pallas_call(
        functools.partial(kernel, n, m),
        out_shape=jax.ShapeDtypeStruct((3, E, E * E), F32),
        in_specs=[anywhere] * 6,
        out_specs=vmem,
        scratch_shapes=[
            pltpu.SMEM((1, 3), jnp.int32),
            pltpu.SMEM((1, 6), jnp.int32),
            pltpu.SMEM((3, 1, 3 * n), F32),
            pltpu.VMEM((3, E, E * E), F32),
            pltpu.VMEM((E, E * E), jnp.int32),
            pltpu.VMEM((3, E, E * E), F32),
            dma((6,)),
            pltpu.VMEM(padded, F32),
            pltpu.VMEM((2,) + padded, F32),
            pltpu.VMEM(inner, F32),
            pltpu.VMEM(inner, F32),
            pltpu.VMEM(inner, F32),
            pltpu.VMEM(inner, F32),
            pltpu.VMEM(inner, F32),
            pltpu.VMEM(inner[1:], jnp.int32),
            pltpu.VMEM((rounds, 4, E, 128), F32),
            pltpu.VMEM((rounds, 4, E, 128), F32),
            pltpu.VMEM((NEWTON, n, 8, 128), F32),
            pltpu.VMEM((NEWTON, m, 8, 128), F32),
            pltpu.VMEM((NEWTON, n, 8, 128), F32),
            pltpu.VMEM((3, n, 8, 128), F32),
            dma((rounds, 4)), dma((rounds, 4)),
            dma((NEWTON, n)), dma((NEWTON, n)),
            dma((NEWTON, m)), dma((NEWTON, m)),
            dma((NEWTON, n)), dma((NEWTON, n)),
        ],
        compiler_params=pltpu.CompilerParams(
            collective_id=0, has_side_effects=True, vmem_limit_bytes=56 * 1024 * 1024
        ),
    )(brick_coords, neighbours, jnp.swapaxes(coarse_inverse, 0, 1), initial_state[0], phases[0], source[0])
    return result[None]


def solution(mesh):
    both = ("group", "space")
    return jax.shard_map(
        functools.partial(shards, mesh.shape["space"], mesh.shape["group"]),
        mesh=mesh,
        in_specs=(
            P(both, None, None, None),
            P(both, None, None),
            P(both, None),
            P(both, None),
            P(both, None, None, None),
            P("group", "space", None),
        ),
        out_specs=P(both, None, None, None),
        check_vma=False,
    )
```
